32 devices in a mesh: days: 2 (over y), blk: 4 (over z), det: 2 (over x), beam: 2 (over core).
Axes of the slice: x: 2, y: 2, z: 4, core: 2. Of those that a mesh axis runs over, the one named last changes fastest.
Arguments:
- solution: float32 [2, 264, 2048], P(None, ('days', 'blk'), 'det'), parts along dimension 1, may hold values from -6 to 6
- residual: float32 [2, 264, 2048], P(None, ('days', 'blk'), 'det'), parts along dimension 1, may hold values from -6 to 6
- direction: float32 [2, 264, 2048], P(None, ('days', 'blk'), 'det'), parts along dimension 1, may hold values from -6 to 6
- legendre: bfloat16 [132, 2048, 4], P('blk', 'det'), may hold values from -0.125 to 0.125
- beam_coef: float32 [2048, 16], P('det', 'beam'), may hold values from 0.5 to 1.5
- prior_weight: float32 [2048], P('det'), may hold values from 1 to 16
- tile_ids: int32 [16, 32], P(('days', 'blk', 'det')), parts along dimension 0, may hold values from 0 to 63, as said below
- interp_weight: bfloat16 [16, 32, 128, 128], P(('days', 'blk', 'det')), parts along dimension 0, may hold values from -0.5 to 0.5
- psi_angle: float32 [16, 32, 128], P(('days', 'blk', 'det')), parts along dimension 0, may hold values from -3.140625 to 3.140625
- noise_coef: float32 [16, 4, 8], P(('days', 'blk', 'det')), parts along dimension 0, may hold values from -0.3 to 0.3
- band_width: int32 [16, 4], P(('days', 'blk', 'det')), parts along dimension 0, may hold values from 1 to 8
Outputs:
- new_solution: float32 [2, 264, 2048], P(None, ('days', 'blk'), 'det'), parts along dimension 1
- new_residual: float32 [2, 264, 2048], P(None, ('days', 'blk'), 'det'), parts along dimension 1
- new_direction: float32 [2, 264, 2048], P(None, ('days', 'blk'), 'det'), parts along dimension 1
The draws below stay inside these ranges and needn't reach their ends.
There are 2 independent parts, one for each index of `days`. The reference program is written for one: setup_inputs(seed, part) draws one part's arguments, and reference() takes and returns one part's arrays. A program takes and returns all parts, laid end to end along the dimension named above; an argument that names none is the same for every part. Nothing has to cross between parts.
Inputs may be any that keep to these rules, and one draw needn't show every extreme that they name: `tile_ids`: tile g lies on cycle g // 16; in every span at most 16 visits read tiles of one cycle, and exactly 16 for some cycle.
All inputs are finite; a program needn't handle non-finite values.
Results may differ from the reference program's by a relative error of at most 0.0024.
Values may be sent and summed in bfloat16 or wider, within the bound.
A program may use at most 64 MiB of HBM per device.

```python
import math
import jax
import jax.numpy as jnp
from jax import lax

L = 2048
M = 132
K = 16
P_SIZE = 2048
TPIX = 128
TILES_DEV = 16
CYCLES = 4
SLOTS = 32
CAP = 16
SEG = 128
SPD = 1024
ND = 4
BW = 8
SPANS = 8
N_BLK = 4
N_DET = 2


def draw_tile_ids(key, part):
    key = jax.random.fold_in(key, 11)
    hot_key, row_key = jax.random.split(key)
    hot_owners = (jax.random.permutation(hot_key, N_BLK) < max(1, N_BLK // 4)).astype(jnp.int32)
    pool_size = N_BLK * CAP
    pool_owner = jnp.arange(pool_size, dtype=jnp.int32) // CAP

    def one_row(row_seed):
        row_keys = jax.random.split(row_seed, 4)
        forced_owner = jax.random.randint(row_keys[0], (), 0, N_BLK)
        scores = jax.random.randint(row_keys[1], (pool_size,), 0, 1024) + 768 * hot_owners[pool_owner]
        scores = jnp.where(pool_owner == forced_owner, -1, scores)
        ranking = scores * pool_size + jnp.arange(pool_size, dtype=jnp.int32)
        ranked_order = jnp.argsort(-ranking, stable=True)
        chosen = pool_owner[ranked_order][:SLOTS - CAP]
        owners = jnp.concatenate([jnp.full((CAP,), forced_owner, jnp.int32), chosen])
        owners = owners[jax.random.permutation(row_keys[2], SLOTS)]
        within = jax.random.randint(row_keys[3], (SLOTS,), 0, TILES_DEV)
        return (owners * TILES_DEV + within).astype(jnp.int32)
    return jax.vmap(one_row)(jax.random.split(row_key, SPANS))


def with_ends(result, stream_key, low, largest):
    index_at = [jax.random.randint(jax.random.fold_in(stream_key, axis), (), 0, length) for axis, length in enumerate(result.shape)]
    longest = result.shape.index(max(result.shape))
    next_to = index_at[:longest] + [(index_at[longest] + 1) % result.shape[longest]] + index_at[longest + 1:]
    return result.at[tuple(index_at)].set(low).at[tuple(next_to)].set(largest)


def levels(stream_key, shape, shards, low, high):
    def one(dim, shards_of):
        draws = jax.random.uniform(jax.random.fold_in(jax.random.fold_in(stream_key, 6), dim), (shards_of,), jnp.float32, low / len(shards), high / len(shards))
        return jnp.repeat(jnp.exp(draws), shape[dim] // shards_of).reshape((-1,) + (1,) * (len(shape) - dim - 1))

    loudness = one(*shards[0])
    for cut in shards[1:]:
        loudness = loudness * one(*cut)
    return loudness


def noise(key, dims, deviation, bound, shards=(), kind=jnp.bfloat16):
    array = jax.random.normal(key, dims, jnp.float32) * deviation
    if len(shards) > 0:
        array = levels(key, dims, shards, -0.22, 0.18) * array
    return jnp.clip(array, min=-bound, max=bound).astype(kind)


def setup_inputs(seed: int = 0, part: int = 0) -> dict:
    streams_of = jax.random.split(jax.random.key(seed), 12)
    part_keys = jax.random.split(jax.random.fold_in(streams_of[11], part), 12)
    return {
        "solution": noise(part_keys[0], (2, M, L), 1.0, 6.0, ((1, 4), (2, 2)), jnp.float32),
        "residual": noise(part_keys[1], (2, M, L), 1.0, 6.0, ((1, 4), (2, 2)), jnp.float32),
        "direction": noise(part_keys[2], (2, M, L), 1.0, 6.0, ((1, 4), (2, 2)), jnp.float32),
        "legendre": noise(streams_of[3], (M, L, CYCLES), L ** -0.5, 0.125, ((0, 4), (1, 2))),
        "beam_coef": jnp.clip(0.5 + 1.0 * jax.random.uniform(streams_of[4], (L, K), jnp.float32) ** levels(streams_of[4], (L, K), ((0, 2), (1, 2)), -0.2, 0.2), 0.5, 1.5),
        "prior_weight": jnp.clip(jnp.exp(math.log(16.0) - 2.7725887 * jax.random.uniform(streams_of[5], (L,), jnp.float32) ** levels(streams_of[5], (L,), ((0, 2),), -0.2, 0.2)), 1.0, 16.0),
        "tile_ids": draw_tile_ids(jax.random.fold_in(jax.random.fold_in(streams_of[11], part), 71), part),
        "interp_weight": noise(part_keys[7], (SPANS, SLOTS, SEG, TPIX), TPIX ** -0.5, 0.5, ((0, 8),)),
        "psi_angle": jnp.clip(jax.random.uniform(part_keys[8], (SPANS, SLOTS, SEG), jnp.float32, -3.140625, 3.140625), -3.140625, 3.140625),
        "noise_coef": jnp.clip(jax.random.uniform(part_keys[9], (SPANS, ND, BW), jnp.float32, -0.3, 0.3) * levels(part_keys[9], (SPANS, ND, BW), ((0, 8),), -0.4, 0.0), -0.3, 0.3),
        "band_width": with_ends(jax.random.randint(part_keys[10], (SPANS, ND), 1, BW + 1), jax.random.fold_in(part_keys[10], 1), 1, BW).astype(jnp.int32),
    }


def beam_basis(angles, mode_ids):
    half_modes = K // 2
    orders = jnp.where(mode_ids < half_modes, mode_ids, mode_ids - half_modes + 1).astype(jnp.float32)
    phases = angles[..., None, :] * orders[:, None]
    return jnp.where((mode_ids < half_modes)[:, None], jnp.cos(phases), jnp.sin(phases))

def fourier_table(orders_total, col_start, col_count):
    order_idx = jnp.arange(orders_total, dtype=jnp.int32)
    pixel_idx = col_start + jnp.arange(col_count, dtype=jnp.int32)
    phase = (order_idx[:, None] * pixel_idx[None, :] % P_SIZE).astype(jnp.float32) * (2.0 * math.pi / P_SIZE)
    norm_scale = 1.0 / math.sqrt(2.0 * orders_total)
    return (jnp.concatenate([jnp.cos(phase), -jnp.sin(phase)], 0) * norm_scale).astype(jnp.bfloat16)

def noise_apply(samples, coefficients, widths):
    lag_ids = jnp.arange(1, BW + 1, dtype=jnp.int32)
    active = (lag_ids <= widths[..., None]).astype(jnp.float32)
    tap_coef = coefficients * active
    center = 1.0 + 2.0 * lax.optimization_barrier(jnp.sum(jnp.abs(tap_coef), axis=-1))
    padding = ((0, 0),) * (samples.ndim - 1) + ((BW, BW),)
    padded = jnp.pad(samples, padding)
    filtered_sum = center[..., None] * samples
    for lag_step in range(1, BW + 1):
        before = padded[..., BW - lag_step:BW - lag_step + SPD]
        after = padded[..., BW + lag_step:BW + lag_step + SPD]
        filtered_sum = filtered_sum + tap_coef[..., lag_step - 1:lag_step] * (before + after)
    return filtered_sum

def reference(solution, residual, direction, legendre, beam_coef, prior_weight, tile_ids, interp_weight, psi_angle, noise_coef, band_width):
    orders_total = direction.shape[1]
    degree_total = direction.shape[2]
    cycle_count = legendre.shape[2]
    tile_count = P_SIZE // TPIX
    scaled = (direction[:, None, :, :] * jnp.transpose(beam_coef)[None, :, None, :]).astype(jnp.bfloat16)
    scaled_parts = scaled.reshape(2, K, orders_total, N_DET, degree_total // N_DET).astype(jnp.float32)
    table_parts = legendre.reshape(orders_total, N_DET, degree_total // N_DET, cycle_count).astype(jnp.float32)
    partial_value = jnp.einsum('ckmdl,mdlr->dckmr', scaled_parts, table_parts)
    partial_value = lax.optimization_barrier(partial_value.astype(jnp.bfloat16)).astype(jnp.float32)
    coeffs = lax.optimization_barrier(jnp.sum(partial_value, axis=0)).astype(jnp.bfloat16)
    cycle_coeffs = jnp.transpose(coeffs, (1, 3, 0, 2)).reshape(K, cycle_count, 2 * orders_total)
    table = fourier_table(orders_total, 0, P_SIZE).astype(jnp.float32)
    cycle_cube = jnp.einsum('krn,np->krp', cycle_coeffs.astype(jnp.float32), table).astype(jnp.bfloat16)
    tiles_all = cycle_cube.reshape(K, cycle_count * tile_count, TPIX)
    picked = tiles_all[:, tile_ids]
    weights = interp_weight.astype(jnp.float32)
    values = jnp.einsum('cstp,kcsp->cskt', weights, picked.astype(jnp.float32))
    mode_ids = jnp.arange(K, dtype=jnp.int32)
    mode_basis = beam_basis(psi_angle, mode_ids)
    signal = lax.optimization_barrier(jnp.sum(mode_basis * values, axis=2))
    span_count = signal.shape[0]
    filtered = noise_apply(signal.reshape(span_count, -1, SPD), noise_coef, band_width).reshape(signal.shape)
    weighted = (mode_basis * filtered[:, :, None, :]).astype(jnp.bfloat16)
    slot_adj = jnp.einsum('cskt,cstp->cskp', weighted.astype(jnp.float32), weights)
    tile_total = jax.ops.segment_sum(slot_adj.reshape(-1, K, TPIX), tile_ids.reshape(-1), num_segments=cycle_count * tile_count)
    cycle_adj = jnp.transpose(tile_total, (1, 0, 2)).reshape(K, cycle_count, P_SIZE).astype(jnp.bfloat16)
    back = jnp.einsum('krp,np->krn', cycle_adj.astype(jnp.float32), table).astype(jnp.bfloat16)
    back = jnp.transpose(back.reshape(K, cycle_count, 2, orders_total), (2, 0, 3, 1))
    spread = jnp.einsum('ckmr,mlr->ckml', back.astype(jnp.float32), legendre.astype(jnp.float32))
    image_field = jnp.einsum('ckml,lk->cml', spread, beam_coef) + prior_weight[None, None, :] * direction
    old_norm = jnp.sum(residual * residual)
    curvature = jnp.sum(direction * image_field)
    step_alpha = old_norm / curvature
    new_solution = solution + step_alpha * direction
    new_residual = residual - step_alpha * image_field
    new_norm = jnp.sum(new_residual * new_residual)
    new_direction = new_residual + new_norm / old_norm * direction
    return (new_solution, new_residual, new_direction)
```

```python
import functools
import math

import jax
import jax.numpy as jnp
import ml_dtypes
import numpy as np
from jax import lax
from jax.experimental import pallas as pl
from jax.experimental.pallas import tpu as pltpu
from jax.sharding import PartitionSpec as P

K = 16
P_SIZE = 2048
TPIX = 128
SPD = 1024
BW = 8
LANES = 128
HALF = 64
F32 = jnp.float32
BF16 = jnp.bfloat16
MESH = pl.DeviceIdType.MESH


def padded_table(blocks, orders):
    total = blocks * orders
    m = np.arange(total, dtype=np.int64)
    j = np.arange(P_SIZE, dtype=np.int64)
    phase = ((m[:, None] * j[None, :]) % P_SIZE).astype(np.float32) * np.float32(
        2.0 * math.pi / P_SIZE
    )
    scale = np.float32(1.0 / math.sqrt(2.0 * total))
    table = np.zeros((blocks, 2, HALF, P_SIZE), np.float32)
    table[:, 0, :orders] = (np.cos(phase) * scale).reshape(blocks, orders, P_SIZE)
    table[:, 1, :orders] = (-np.sin(phase) * scale).reshape(blocks, orders, P_SIZE)
    return table.reshape(blocks * LANES, P_SIZE).astype(ml_dtypes.bfloat16)


def loop(count, step):
    if count <= 8:
        for i in range(count):
            step(i)
    else:
        lax.fori_loop(0, count, lambda i, c: (step(i), c)[1], 0)


def mult(x, m):
    return x if isinstance(x, int) else pl.multiple_of(x, m)


def dot_nt(a, b):
    return lax.dot_general(a, b, (((1,), (1,)), ((), ())), preferred_element_type=F32)


def dot_nn(a, b):
    return lax.dot_general(a, b, (((1,), (0,)), ((), ())), preferred_element_type=F32)


def dot_tn(a, b):
    return lax.dot_general(a, b, (((0,), (0,)), ((), ())), preferred_element_type=F32)


def split2(x):
    hi = x.astype(BF16)
    return hi, (x - hi.astype(F32)).astype(BF16)


def kernel(
    nb, nd, mo, rr, kl, sol_h, res_h, dir_h, leg_h, beam_v, prior_v, ids_s, ids_v, w_h, psi_v,
    noise_s, band_s, table_h, osol_h, ores_h, odir_h,
    sol_v, res_v, dir_v, leg_v, legf, w_v, table_v, yhi, ylo, part, asend, arecv, coef, brecv,
    tiles, basis, prod, sigs, filt, sadj, tt, adj, dsend, drecv, erecv, backf, img, gsend, grecv,
    in_sem, out_sem, b_sem, a_ss, a_rs, c_sem, d_ss, d_rs, e_ss, e_rs, g_ss, g_rs,
):
    n = nb * nd
    days, blk = lax.axis_index("days"), lax.axis_index("blk")
    det, beam = lax.axis_index("det"), lax.axis_index("beam")
    me = blk * nd + det
    kr = rr * kl
    krd = kr // nd
    lt_n = beam_v.shape[1] // LANES
    slots = w_v.shape[0]
    tile_n = P_SIZE // TPIX

    def peer(i):
        t = lax.rem(me + i, n)
        return t, lax.div(t, nd), lax.rem(t, nd)

    loads = [
        pltpu.make_async_copy(src, dst, in_sem.at[i])
        for i, (src, dst) in enumerate(
            [(dir_h, dir_v), (leg_h, leg_v), (table_h, table_v), (w_h, w_v), (res_h, res_v), (sol_h, sol_v)]
        )
    ]
    for copy in loads:
        copy.start()

    barrier = pltpu.get_barrier_semaphore()

    def greet(i):
        _, b, d = peer(i + 1)
        pl.semaphore_signal(barrier, inc=1, device_id=(days, b, d, beam), device_id_type=MESH)

    loop(n - 1, greet)
    for i in range(nd):
        pl.semaphore_signal(
            barrier, inc=1, device_id=(days, blk, lax.rem(det + i, nd), 1 - beam), device_id_type=MESH
        )

    def rows(start, stride):
        return pl.ds(start, mo, stride=stride)

    psi = psi_v[...]
    c1, s1 = jnp.cos(psi), jnp.sin(psi)
    ck, sk = jnp.ones_like(psi), jnp.zeros_like(psi)
    first = beam == 0
    for k in range(kl):
        cn, sn = ck * c1 - sk * s1, sk * c1 + ck * s1
        basis[pl.ds(k, slots, stride=kl), :] = jnp.where(first, ck, sn)
        ck, sk = cn, sn

    loads[0].wait()
    loads[1].wait()
    legf[...] = leg_v[...].astype(F32)
    brecv[beam] = beam_v[...]
    bh = beam_v[...].astype(BF16).astype(F32)
    lhs = jnp.concatenate([bh, beam_v[...] - bh], axis=0).astype(BF16)
    lane = lax.broadcasted_iota(jnp.int32, (kl, LANES), 1)
    keep = lax.rem(lane, HALF) < mo

    def forward(pair):
        for h in range(2):
            r = pair * 2 + h
            for lt in range(lt_n):
                lg = legf[rows(lt * rr + r, lt_n * rr), :]
                for c in range(2):
                    y = dir_v[rows(lt * 2 + c, lt_n * 2), :] * lg
                    yh, yl = split2(y)
                    at = mult(r * LANES + c * HALF, HALF)
                    yhi[pl.ds(at, mo), lt * LANES : (lt + 1) * LANES] = yh
                    ylo[pl.ds(at, mo), lt * LANES : (lt + 1) * LANES] = yl
        span = pl.ds(mult(pair * 2 * LANES, 2 * LANES), 2 * LANES)
        oh = dot_nt(lhs, yhi[span, :])
        ol = dot_nt(lhs, ylo[span, :])
        total = oh[:kl] + (oh[kl:] + ol[:kl])
        for h in range(2):
            at = mult((pair * 2 + h) * kl, kl)
            part[pl.ds(at, kl), :] = jnp.where(keep, total[:, h * LANES : (h + 1) * LANES], 0.0)

    loop(rr // 2, forward)
    asend[...] = part[...].astype(BF16)
    arecv[me] = asend[...]

    pl.semaphore_wait(barrier, n - 1 + nd)

    def a_send(i):
        _, b, d = peer(i + 1)
        pltpu.make_async_remote_copy(
            asend, arecv.at[me], a_ss, a_rs, device_id=(days, b, d, beam), device_id_type=MESH
        ).start()

    loop(n - 1, a_send)
    sister = (days, blk, det, 1 - beam)
    b_copy = pltpu.make_async_remote_copy(
        beam_v, brecv.at[beam], b_sem.at[0], b_sem.at[1], device_id=sister, device_id_type=MESH
    )
    b_copy.start()

    def wait_all(buffer, send_sem, recv_sem):
        some = buffer.at[pl.ds(0, n - 1)]
        pltpu.make_async_copy(some, some, recv_sem).wait()
        pltpu.make_async_copy(some, some, send_sem).wait()

    wait_all(arecv, a_ss, a_rs)

    def add_det(b):
        total = arecv[b * nd].astype(F32)
        for d in range(1, nd):
            total = total + arecv[b * nd + d].astype(F32)
        coef[:, pl.ds(mult(b * LANES, LANES), LANES)] = total.astype(BF16)

    loop(nb, add_det)

    loads[2].wait()
    width = 512
    lhs_c = coef[...]

    def to_pixels(jc):
        out = dot_nn(lhs_c, table_v[:, pl.ds(mult(jc * width, width), width)])
        out = out.astype(BF16).astype(F32)
        for r in range(rr):
            for q in range(width // TPIX):
                tiles[r * tile_n + jc * (width // TPIX) + q] = out[
                    r * kl : (r + 1) * kl, q * TPIX : (q + 1) * TPIX
                ]

    loop(P_SIZE // width, to_pixels)
    loads[3].wait()
    for s in range(slots):
        tile = tiles[ids_s[0, s]].astype(BF16)
        at = slice(s * kl, (s + 1) * kl)
        prod[at, :] = basis[at, :] * dot_nt(tile, w_v[s])
    sig = prod[pl.ds(0, slots, stride=kl), :]
    for k in range(1, kl):
        sig = sig + prod[pl.ds(k, slots, stride=kl), :]
    sigs[beam] = sig
    c_copy = pltpu.make_async_remote_copy(
        sigs.at[beam], sigs.at[beam], c_sem.at[0], c_sem.at[1], device_id=sister, device_id_type=MESH
    )
    c_copy.start()
    c_copy.wait()

    srow = SPD // LANES
    row8 = lax.broadcasted_iota(jnp.int32, (srow, LANES), 0)
    lane8 = lax.broadcasted_iota(jnp.int32, (srow, LANES), 1)
    for d in range(slots // srow):
        at = slice(d * srow, (d + 1) * srow)
        x = sigs[0, at, :] + sigs[1, at, :]
        prev = jnp.where(row8 == 0, 0.0, pltpu.roll(x, 1, 0))
        nxt = jnp.where(row8 == srow - 1, 0.0, pltpu.roll(x, srow - 1, 0))
        center = jnp.float32(0.0)
        total = jnp.zeros_like(x)
        for i in range(1, BW + 1):
            tap = jnp.where(i <= band_s[0, d], noise_s[0, d, i - 1], 0.0)
            center = center + jnp.abs(tap)
            before = jnp.where(lane8 < i, pltpu.roll(prev, i, 1), pltpu.roll(x, i, 1))
            after = jnp.where(
                lane8 >= LANES - i, pltpu.roll(nxt, LANES - i, 1), pltpu.roll(x, LANES - i, 1)
            )
            total = total + tap * (before + after)
        filt[at, :] = (1.0 + 2.0 * center) * x + total

    for s in range(slots):
        at = slice(s * kl, (s + 1) * kl)
        wt = (basis[at, :] * filt[s : s + 1, :]).astype(BF16)
        sadj[at, :] = dot_nn(wt, w_v[s])
    tiles_all = rr * tile_n
    hot = (
        lax.broadcasted_iota(jnp.int32, (tiles_all, slots), 0) == ids_v[...]
    ).astype(F32).astype(BF16)
    xs = jnp.concatenate([sadj[pl.ds(k, slots, stride=kl), :] for k in range(kl)], axis=1)
    xh, xl = split2(xs)
    ts = dot_nn(hot, xh) + dot_nn(hot, xl)
    for k in range(kl):
        tt[pl.ds(k, tiles_all, stride=kl), :] = ts[:, k * TPIX : (k + 1) * TPIX]
    for r in range(rr):
        for q in range(tile_n):
            g = r * tile_n + q
            adj[r * kl : (r + 1) * kl, q * TPIX : (q + 1) * TPIX] = tt[g * kl : (g + 1) * kl, :]
    ah, al = split2(adj[...])
    lhs_a = jnp.concatenate([ah, al], axis=0)

    def to_orders(pair):
        out = dot_nt(lhs_a, table_v[pl.ds(mult(pair * 2 * LANES, 2 * LANES), 2 * LANES), :])
        out = out[:kr] + out[kr:]
        for h in range(2):
            dsend[pair * 2 + h] = out[:, h * LANES : (h + 1) * LANES]

    loop(nb // 2, to_orders)

    def my_rows(d):
        return pl.ds(mult(d * krd, krd), krd)

    def d_send(i):
        _, b, d = peer(i + 1)
        pltpu.make_async_remote_copy(
            dsend.at[b, my_rows(d)], drecv.at[me], d_ss, d_rs,
            device_id=(days, b, d, beam), device_id_type=MESH,
        ).start()

    loop(n - 1, d_send)
    drecv[me] = dsend[blk, my_rows(det), :]
    wait_all(drecv, d_ss, d_rs)
    back = drecv[0]
    for i in range(1, n):
        back = back + drecv[i]
    erecv[beam, det] = back.astype(BF16)
    e_copies = []
    for bm in range(2):
        for i in range(nd):
            if bm == 0 and i == 0:
                continue
            mine = erecv.at[beam, det]
            e_copies.append(
                pltpu.make_async_remote_copy(
                    mine, mine, e_ss.at[len(e_copies)], e_rs.at[len(e_copies)],
                    device_id=(days, blk, lax.rem(det + i, nd), beam if bm == 0 else 1 - beam),
                    device_id_type=MESH,
                )
            )
    for copy in e_copies:
        copy.start()
    loads[4].wait()
    loads[5].wait()
    b_copy.wait()
    bm_all = jnp.concatenate([brecv[0], brecv[1]], axis=0)
    gh = bm_all.astype(BF16)
    rhs_b = jnp.concatenate([gh, (bm_all - gh.astype(F32)).astype(BF16)], axis=0)
    for copy in e_copies:
        copy.wait()
    for bm in range(2):
        for d in range(nd):
            backf[bm, d * krd : (d + 1) * krd, :] = erecv[bm, d].astype(F32)

    for lt in range(lt_n):
        for c in range(2):
            at = lt * 2 + c
            img[rows(at, lt_n * 2), :] = prior_v[lt : lt + 1, :] * dir_v[rows(at, lt_n * 2), :]

    def to_image(r):
        at = pl.ds(mult(r * kl, kl), kl)
        b0, b1 = backf[0, at, :], backf[1, at, :]
        lb = jnp.concatenate([b0, b1, b0, b1], axis=0).astype(BF16)
        g = dot_tn(lb, rhs_b)
        for lt in range(lt_n):
            lg = legf[rows(lt * rr + r, lt_n * rr), :]
            for c in range(2):
                to = rows(lt * 2 + c, lt_n * 2)
                img[to, :] = img[to, :] + lg * g[
                    c * HALF : c * HALF + mo, lt * LANES : (lt + 1) * LANES
                ]

    loop(rr, to_image)

    acc = None
    for q in range(lt_n * 2):
        at = rows(q, lt_n * 2)
        rv, dv, iv = res_v[at, :], dir_v[at, :], img[at, :]
        terms = [rv * rv, dv * iv, rv * iv, iv * iv]
        acc = terms if acc is None else [a + t for a, t in zip(acc, terms)]
    gsend[...] = jnp.zeros_like(gsend)
    for i, a in enumerate(acc):
        gsend[i : i + 1, :] = jnp.sum(a, axis=0, keepdims=True)

    def g_send(i):
        _, b, d = peer(i + 1)
        pltpu.make_async_remote_copy(
            gsend, grecv.at[me], g_ss, g_rs, device_id=(days, b, d, beam), device_id_type=MESH
        ).start()

    loop(n - 1, g_send)
    grecv[me] = gsend[...]
    wait_all(grecv, g_ss, g_rs)
    tot = grecv[0]
    for i in range(1, n):
        tot = tot + grecv[i]
    sums = jnp.sum(tot, axis=1, keepdims=True)
    rr_sum, di_sum, ri_sum, ii_sum = (sums[i : i + 1, :] for i in range(4))
    alpha = rr_sum / di_sum
    new_norm = rr_sum - 2.0 * alpha * ri_sum + alpha * alpha * ii_sum
    beta = new_norm / rr_sum
    dv = dir_v[...]
    nr = res_v[...] - alpha * img[...]
    res_v[...] = nr
    o_res = pltpu.make_async_copy(res_v, ores_h, out_sem.at[0])
    o_res.start()
    sol_v[...] = sol_v[...] + alpha * dv
    o_sol = pltpu.make_async_copy(sol_v, osol_h, out_sem.at[1])
    o_sol.start()
    img[...] = nr + beta * dv
    o_dir = pltpu.make_async_copy(img, odir_h, out_sem.at[2])
    o_dir.start()
    o_res.wait()
    o_sol.wait()
    o_dir.wait()


def flat(x):
    a, m, l = x.shape
    y = jnp.transpose(x, (1, 0, 2)).reshape(m, a, l // LANES, LANES)
    return jnp.transpose(y, (0, 2, 1, 3)).reshape(m * l // LANES * a, LANES)


def unflat(y, a, m, l):
    x = jnp.transpose(y.reshape(m, l // LANES, a, LANES), (0, 2, 1, 3)).reshape(m, a, l)
    return jnp.transpose(x, (1, 0, 2))


def body(
    nb, nd, table, solution, residual, direction, legendre, beam_coef, prior_weight, tile_ids,
    interp_weight, psi_angle, noise_coef, band_width,
):
    _, mo, ll = direction.shape
    rr = legendre.shape[2]
    kl = beam_coef.shape[1]
    slots = tile_ids.shape[1]
    n = nb * nd
    kr = rr * kl
    frows = 2 * mo * ll // LANES
    lrows = rr * mo * ll // LANES
    tiles_all = rr * (P_SIZE // TPIX)
    any_spec = pl.BlockSpec(memory_space=pl.ANY)
    vmem = pl.BlockSpec(memory_space=pltpu.VMEM)
    smem = pl.BlockSpec(memory_space=pltpu.SMEM)
    V = pltpu.VMEM
    dma = pltpu.SemaphoreType.DMA
    flat_shape = jax.ShapeDtypeStruct((frows, LANES), F32)
    outs = pl.pallas_call(
        functools.partial(kernel, nb, nd, mo, rr, kl),
        out_shape=(flat_shape,) * 3,
        in_specs=[any_spec] * 4 + [vmem, vmem, smem, vmem, any_spec, vmem, smem, smem, any_spec],
        out_specs=(any_spec,) * 3,
        scratch_shapes=[
            V((frows, LANES), F32), V((frows, LANES), F32), V((frows, LANES), F32),
            V((lrows, LANES), BF16), V((lrows, LANES), F32),
            V((slots, LANES, TPIX), BF16), V((nb * LANES, P_SIZE), BF16),
            V((rr * LANES, ll), BF16), V((rr * LANES, ll), BF16),
            V((kr, LANES), F32), V((kr, LANES), BF16), V((n, kr, LANES), BF16),
            V((kr, nb * LANES), BF16), V((2, kl, ll), F32),
            V((tiles_all, kl, TPIX), F32), V((slots * kl, LANES), F32), V((slots * kl, LANES), F32),
            V((2, slots, LANES), F32), V((slots, LANES), F32), V((slots * kl, TPIX), F32),
            V((tiles_all * kl, TPIX), F32), V((kr, P_SIZE), F32),
            V((nb, kr, LANES), F32), V((n, kr // nd, LANES), F32),
            V((2, nd, kr // nd, LANES), BF16), V((2, kr, LANES), F32),
            V((frows, LANES), F32), V((8, LANES), F32), V((n, 8, LANES), F32),
            dma((6,)), dma((3,)), dma((2,)), dma, dma, dma((2,)), dma, dma,
            dma((2 * nd - 1,)), dma((2 * nd - 1,)), dma, dma,
        ],
        compiler_params=pltpu.CompilerParams(
            collective_id=0, has_side_effects=True, vmem_limit_bytes=60 * 1024 * 1024
        ),
        name="cg_step",
    )(
        flat(solution), flat(residual), flat(direction), flat(jnp.transpose(legendre, (2, 0, 1))),
        jnp.transpose(beam_coef), prior_weight.reshape(ll // LANES, LANES), tile_ids, tile_ids,
        interp_weight[0], psi_angle[0], noise_coef, band_width, table,
    )
    return tuple(unflat(o, 2, mo, ll) for o in outs)


def solution(mesh):
    nb, nd = mesh.shape["blk"], mesh.shape["det"]
    field = P(None, ("days", "blk"), "det")
    spans = ("days", "blk", "det")
    in_specs = (
        field, field, field, P("blk", "det", None), P("det", "beam"), P("det"), P(spans, None),
        P(spans, None, None, None), P(spans, None, None), P(spans, None, None), P(spans, None),
    )

    def run(*args):
        orders = args[2].shape[1] // (nb * mesh.shape["days"])
        table = padded_table(nb, orders)
        return jax.shard_map(
            functools.partial(body, nb, nd, jnp.asarray(table)),
            mesh=mesh, in_specs=in_specs, out_specs=(field,) * 3, check_vma=False,
        )(*args)

    return run
```

```python
import functools
import math

import jax
import jax.numpy as jnp
import ml_dtypes
import numpy as np
from jax import lax
from jax.experimental import pallas as pl
from jax.experimental.pallas import tpu as pltpu
from jax.sharding import PartitionSpec as P

K = 16
P_SIZE = 2048
TPIX = 128
SPD = 1024
BW = 8
LANES = 128
HALF = 64
F32 = jnp.float32
BF16 = jnp.bfloat16
MESH = pl.DeviceIdType.MESH


def padded_table(blocks, orders):
    total = blocks * orders
    m = np.arange(total, dtype=np.int64)
    j = np.arange(P_SIZE, dtype=np.int64)
    phase = ((m[:, None] * j[None, :]) % P_SIZE).astype(np.float32) * np.float32(
        2.0 * math.pi / P_SIZE
    )
    scale = np.float32(1.0 / math.sqrt(2.0 * total))
    table = np.zeros((blocks, 2, HALF, P_SIZE), np.float32)
    table[:, 0, :orders] = (np.cos(phase) * scale).reshape(blocks, orders, P_SIZE)
    table[:, 1, :orders] = (-np.sin(phase) * scale).reshape(blocks, orders, P_SIZE)
    return table.reshape(blocks * LANES, P_SIZE).astype(ml_dtypes.bfloat16)


def loop(count, step):
    if count <= 8:
        for i in range(count):
            step(i)
    else:
        lax.fori_loop(0, count, lambda i, c: (step(i), c)[1], 0)


def mult(x, m):
    return x if isinstance(x, int) else pl.multiple_of(x, m)


def dot_nt(a, b):
    return lax.dot_general(a, b, (((1,), (1,)), ((), ())), preferred_element_type=F32)


def dot_nn(a, b):
    return lax.dot_general(a, b, (((1,), (0,)), ((), ())), preferred_element_type=F32)


def dot_tn(a, b):
    return lax.dot_general(a, b, (((0,), (0,)), ((), ())), preferred_element_type=F32)


def split2(x):
    hi = x.astype(BF16)
    return hi, (x - hi.astype(F32)).astype(BF16)


def kernel(
    nb, nd, mo, rr, kl, two, res_h, dir_h, leg_h, beam_v, prior_v, ids_s, ids_v, w_h, psi_v,
    noise_s, band_s, table_h, back_h, img, sums_v,
    res_v, dir_v, leg_v, legf, w_v, table_v, back_s, yhi, ylo, part, asend, arecv, coef, brecv,
    tiles, basis, prod, sigs, filt, sadj, tt, adj, dsend, drecv, erecv, backf, gsend, grecv,
    in_sem, b_sem, a_ss, a_rs, c_sem, d_ss, d_rs, e_ss, e_rs, g_ss, g_rs,
):
    n = nb * nd
    back_v = back_s if two else None
    days, blk = lax.axis_index("days"), lax.axis_index("blk")
    det, beam = lax.axis_index("det"), lax.axis_index("beam")
    me = blk * nd + det
    kr = rr * kl
    lt_n = beam_v.shape[1] // LANES
    slots = w_v.shape[0]
    tile_n = P_SIZE // TPIX

    def peer(i):
        t = lax.rem(me + i, n)
        return t, lax.div(t, nd), lax.rem(t, nd)

    loads = [
        pltpu.make_async_copy(src, dst, in_sem.at[i])
        for i, (src, dst) in enumerate(
            [(dir_h, dir_v), (leg_h, leg_v), (table_h, table_v), (w_h, w_v), (res_h, res_v)]
        )
    ]
    if two:
        loads.append(pltpu.make_async_copy(back_h, back_s, in_sem.at[5]))
    for copy in loads:
        copy.start()

    barrier = pltpu.get_barrier_semaphore()

    def greet(i):
        _, b, d = peer(i + 1)
        pl.semaphore_signal(barrier, inc=1, device_id=(days, b, d, beam), device_id_type=MESH)

    loop(n - 1, greet)
    pl.semaphore_signal(barrier, inc=1, device_id=(days, blk, det, 1 - beam), device_id_type=MESH)

    def rows(start, stride):
        return pl.ds(start, mo, stride=stride)

    loads[0].wait()
    loads[1].wait()
    legf[...] = leg_v[...].astype(F32)
    brecv[beam] = beam_v[...]
    bh = beam_v[...].astype(BF16).astype(F32)
    lhs = jnp.concatenate([bh, beam_v[...] - bh], axis=0).astype(BF16)
    lane = lax.broadcasted_iota(jnp.int32, (kl, LANES), 1)
    keep = lax.rem(lane, HALF) < mo

    def forward(pair):
        for h in range(2):
            r = pair * 2 + h
            for lt in range(lt_n):
                lg = legf[rows(lt * rr + r, lt_n * rr), :]
                for c in range(2):
                    y = dir_v[rows(lt * 2 + c, lt_n * 2), :] * lg
                    yh, yl = split2(y)
                    at = mult(r * LANES + c * HALF, HALF)
                    yhi[pl.ds(at, mo), lt * LANES : (lt + 1) * LANES] = yh
                    ylo[pl.ds(at, mo), lt * LANES : (lt + 1) * LANES] = yl
        span = pl.ds(mult(pair * 2 * LANES, 2 * LANES), 2 * LANES)
        oh = dot_nt(yhi[span, :], lhs).T
        ol = dot_nt(ylo[span, :], lhs).T
        total = oh[:kl] + (oh[kl:] + ol[:kl])
        for h in range(2):
            at = mult((pair * 2 + h) * kl, kl)
            part[pl.ds(at, kl), :] = jnp.where(keep, total[:, h * LANES : (h + 1) * LANES], 0.0)

    loop(rr // 2, forward)
    asend[...] = part[...].astype(BF16)
    arecv[me] = asend[...]

    pl.semaphore_wait(barrier, n)

    def a_send(i):
        _, b, d = peer(i + 1)
        pltpu.make_async_remote_copy(
            asend, arecv.at[me], a_ss, a_rs, device_id=(days, b, d, beam), device_id_type=MESH
        ).start()

    loop(n - 1, a_send)
    sister = (days, blk, det, 1 - beam)
    b_copy = pltpu.make_async_remote_copy(
        beam_v, brecv.at[beam], b_sem.at[0], b_sem.at[1], device_id=sister, device_id_type=MESH
    )
    b_copy.start()

    def wait_all(buffer, send_sem, recv_sem):
        some = buffer.at[pl.ds(0, n - 1)]
        pltpu.make_async_copy(some, some, recv_sem).wait()
        pltpu.make_async_copy(some, some, send_sem).wait()

    psi = psi_v[...]
    c1, s1 = jnp.cos(psi), jnp.sin(psi)
    ck, sk = jnp.ones_like(psi), jnp.zeros_like(psi)
    first = beam == 0
    for k in range(kl):
        cn, sn = ck * c1 - sk * s1, sk * c1 + ck * s1
        basis[pl.ds(k, slots, stride=kl), :] = jnp.where(first, ck, sn)
        ck, sk = cn, sn

    wait_all(arecv, a_ss, a_rs)

    def add_det(b):
        total = arecv[b * nd].astype(F32)
        for d in range(1, nd):
            total = total + arecv[b * nd + d].astype(F32)
        coef[:, pl.ds(mult(b * LANES, LANES), LANES)] = total.astype(BF16)

    loop(nb, add_det)

    loads[2].wait()
    width = 512
    lhs_c = coef[...]

    def to_pixels(jc):
        out = dot_nn(lhs_c, table_v[:, pl.ds(mult(jc * width, width), width)])
        out = out.astype(BF16).astype(F32)
        for r in range(rr):
            for q in range(width // TPIX):
                tiles[r * tile_n + jc * (width // TPIX) + q] = out[
                    r * kl : (r + 1) * kl, q * TPIX : (q + 1) * TPIX
                ]

    loop(P_SIZE // width, to_pixels)
    loads[3].wait()
    for s in range(slots):
        tile = tiles[ids_s[0, s]].astype(BF16)
        at = slice(s * kl, (s + 1) * kl)
        prod[at, :] = basis[at, :] * dot_nt(tile, w_v[s])
    sig = prod[pl.ds(0, slots, stride=kl), :]
    for k in range(1, kl):
        sig = sig + prod[pl.ds(k, slots, stride=kl), :]
    sigs[beam] = sig
    c_copy = pltpu.make_async_remote_copy(
        sigs.at[beam], sigs.at[beam], c_sem.at[0], c_sem.at[1], device_id=sister, device_id_type=MESH
    )
    c_copy.start()
    c_copy.wait()

    srow = SPD // LANES
    row8 = lax.broadcasted_iota(jnp.int32, (srow, LANES), 0)
    lane8 = lax.broadcasted_iota(jnp.int32, (srow, LANES), 1)
    for d in range(slots // srow):
        at = slice(d * srow, (d + 1) * srow)
        x = sigs[0, at, :] + sigs[1, at, :]
        prev = jnp.where(row8 == 0, 0.0, pltpu.roll(x, 1, 0))
        nxt = jnp.where(row8 == srow - 1, 0.0, pltpu.roll(x, srow - 1, 0))
        center = jnp.float32(0.0)
        total = jnp.zeros_like(x)
        for i in range(1, BW + 1):
            tap = jnp.where(i <= band_s[0, d], noise_s[0, d, i - 1], 0.0)
            center = center + jnp.abs(tap)
            before = jnp.where(lane8 < i, pltpu.roll(prev, i, 1), pltpu.roll(x, i, 1))
            after = jnp.where(
                lane8 >= LANES - i, pltpu.roll(nxt, LANES - i, 1), pltpu.roll(x, LANES - i, 1)
            )
            total = total + tap * (before + after)
        filt[at, :] = (1.0 + 2.0 * center) * x + total

    for s in range(slots):
        at = slice(s * kl, (s + 1) * kl)
        wt = (basis[at, :] * filt[s : s + 1, :]).astype(BF16)
        sadj[at, :] = dot_nn(wt, w_v[s])
    tiles_all = rr * tile_n
    hot = (
        lax.broadcasted_iota(jnp.int32, (tiles_all, slots), 0) == ids_v[...]
    ).astype(F32).astype(BF16)
    xs = jnp.concatenate([sadj[pl.ds(k, slots, stride=kl), :] for k in range(kl)], axis=1)
    xh, xl = split2(xs)
    ts = dot_nn(hot, xh) + dot_nn(hot, xl)
    for k in range(kl):
        tt[pl.ds(k, tiles_all, stride=kl), :] = ts[:, k * TPIX : (k + 1) * TPIX]
    for r in range(rr):
        for q in range(tile_n):
            g = r * tile_n + q
            adj[r * kl : (r + 1) * kl, q * TPIX : (q + 1) * TPIX] = tt[g * kl : (g + 1) * kl, :]
    if two:
        loads[5].wait()
    ah, al = split2(adj[...])
    lhs_a = jnp.concatenate([ah, al], axis=0)

    def to_orders(pair):
        span = pl.ds(mult(pair * 2 * LANES, 2 * LANES), 2 * LANES)
        if back_v is None:
            out = dot_nt(lhs_a, table_v[span, :])
        else:
            out = dot_nn(lhs_a, back_v[:, span])
        out = out[:kr] + out[kr:]
        for h in range(2):
            dsend[pair * 2 + h] = out[:, h * LANES : (h + 1) * LANES].astype(BF16)

    loop(nb // 2, to_orders)

    def d_send(i):
        _, b, d = peer(i + 1)
        pltpu.make_async_remote_copy(
            dsend.at[b], drecv.at[me], d_ss, d_rs,
            device_id=(days, b, d, beam), device_id_type=MESH,
        ).start()

    loop(n - 1, d_send)
    drecv[me] = dsend[blk]
    wait_all(drecv, d_ss, d_rs)
    back = drecv[0].astype(F32)
    for i in range(1, n):
        back = back + drecv[i].astype(F32)
    erecv[beam] = back.astype(BF16)
    e_copies = [
        pltpu.make_async_remote_copy(
            erecv.at[beam], erecv.at[beam], e_ss, e_rs, device_id=sister, device_id_type=MESH
        )
    ]
    for copy in e_copies:
        copy.start()
    loads[4].wait()
    b_copy.wait()
    bm_all = jnp.concatenate([brecv[0], brecv[1]], axis=0)
    gh = bm_all.astype(BF16)
    rhs_b = jnp.concatenate([gh, (bm_all - gh.astype(F32)).astype(BF16)], axis=0)
    for copy in e_copies:
        copy.wait()
    for bm in range(2):
        backf[bm] = erecv[bm].astype(F32)

    for lt in range(lt_n):
        for c in range(2):
            at = lt * 2 + c
            img[rows(at, lt_n * 2), :] = prior_v[lt : lt + 1, :] * dir_v[rows(at, lt_n * 2), :]

    def to_image(r):
        at = pl.ds(mult(r * kl, kl), kl)
        b0, b1 = backf[0, at, :], backf[1, at, :]
        lb = jnp.concatenate([b0, b1, b0, b1], axis=0).astype(BF16)
        g = dot_tn(lb, rhs_b)
        for lt in range(lt_n):
            lg = legf[rows(lt * rr + r, lt_n * rr), :]
            for c in range(2):
                to = rows(lt * 2 + c, lt_n * 2)
                img[to, :] = img[to, :] + lg * g[
                    c * HALF : c * HALF + mo, lt * LANES : (lt + 1) * LANES
                ]

    loop(rr, to_image)

    acc = None
    for q in range(lt_n * 2):
        at = rows(q, lt_n * 2)
        rv, dv, iv = res_v[at, :], dir_v[at, :], img[at, :]
        terms = [rv * rv, dv * iv, rv * iv, iv * iv]
        acc = terms if acc is None else [a + t for a, t in zip(acc, terms)]
    gsend[...] = jnp.zeros_like(gsend)
    for i, a in enumerate(acc):
        gsend[i : i + 1, :] = jnp.sum(a, axis=0, keepdims=True)

    def g_send(i):
        _, b, d = peer(i + 1)
        pltpu.make_async_remote_copy(
            gsend, grecv.at[me], g_ss, g_rs, device_id=(days, b, d, beam), device_id_type=MESH
        ).start()

    loop(n - 1, g_send)
    grecv[me] = gsend[...]
    wait_all(grecv, g_ss, g_rs)
    tot = grecv[0]
    for i in range(1, n):
        tot = tot + grecv[i]
    sums_v[...] = tot


def update_kernel(sol_v, res_v, dir_v, img_v, sums_v, osol_v, ores_v, odir_v):
    sums = jnp.sum(sums_v[...], axis=1, keepdims=True)
    rr_sum, di_sum, ri_sum, ii_sum = (sums[i : i + 1, :] for i in range(4))
    alpha = rr_sum / di_sum
    new_norm = rr_sum - 2.0 * alpha * ri_sum + alpha * alpha * ii_sum
    beta = new_norm / rr_sum
    dv = dir_v[...]
    nr = res_v[...] - alpha * img_v[...]
    ores_v[...] = nr
    osol_v[...] = sol_v[...] + alpha * dv
    odir_v[...] = nr + beta * dv


def flat(x):
    a, m, l = x.shape
    y = jnp.transpose(x, (1, 0, 2)).reshape(m, a, l // LANES, LANES)
    return jnp.transpose(y, (0, 2, 1, 3)).reshape(m * l // LANES * a, LANES)


def unflat(y, a, m, l):
    x = jnp.transpose(y.reshape(m, l // LANES, a, LANES), (0, 2, 1, 3)).reshape(m, a, l)
    return jnp.transpose(x, (1, 0, 2))


def body(
    nb, nd, table_np, solution, residual, direction, legendre, beam_coef, prior_weight, tile_ids,
    interp_weight, psi_angle, noise_coef, band_width,
):
    _, mo, ll = direction.shape
    table = jnp.asarray(table_np)
    two = nb <= 8
    rr = legendre.shape[2]
    kl = beam_coef.shape[1]
    slots = tile_ids.shape[1]
    n = nb * nd
    kr = rr * kl
    frows = 2 * mo * ll // LANES
    lrows = rr * mo * ll // LANES
    tiles_all = rr * (P_SIZE // TPIX)
    any_spec = pl.BlockSpec(memory_space=pl.ANY)
    vmem = pl.BlockSpec(memory_space=pltpu.VMEM)
    smem = pl.BlockSpec(memory_space=pltpu.SMEM)
    V = pltpu.VMEM
    dma = pltpu.SemaphoreType.DMA
    flat_shape = jax.ShapeDtypeStruct((frows, LANES), F32)
    sol, res, dirn = flat(solution), flat(residual), flat(direction)
    scratch = [
        V((frows, LANES), F32), V((frows, LANES), F32),
        V((lrows, LANES), BF16), V((lrows, LANES), F32),
        V((slots, LANES, TPIX), BF16), V((nb * LANES, P_SIZE), BF16),
        V((P_SIZE, nb * LANES) if two else (16, LANES), BF16),
        V((rr * LANES, ll), BF16), V((rr * LANES, ll), BF16),
        V((kr, LANES), F32), V((kr, LANES), BF16), V((n, kr, LANES), BF16),
        V((kr, nb * LANES), BF16), V((2, kl, ll), F32),
        V((tiles_all, kl, TPIX), F32), V((slots * kl, LANES), F32), V((slots * kl, LANES), F32),
        V((2, slots, LANES), F32), V((slots, LANES), F32), V((slots * kl, TPIX), F32),
        V((tiles_all * kl, TPIX), F32), V((kr, P_SIZE), F32),
        V((nb, kr, LANES), BF16), V((n, kr, LANES), BF16),
        V((2, kr, LANES), BF16), V((2, kr, LANES), F32),
        V((8, LANES), F32), V((n, 8, LANES), F32),
        dma((6,)), dma((2,)), dma, dma, dma((2,)), dma, dma,
        dma, dma, dma, dma,
    ]
    held = sum(
        math.prod(v.shape) * v.dtype.itemsize for v in scratch if hasattr(v, 'dtype') and getattr(v, 'memory_space', None) == V)
    grant = held + held // 8 + 6 * 1024 * 1024
    image, sums = pl.pallas_call(
        functools.partial(kernel, nb, nd, mo, rr, kl, two),
        out_shape=(flat_shape, jax.ShapeDtypeStruct((8, LANES), F32)),
        in_specs=[any_spec] * 3 + [vmem, vmem, smem, vmem, any_spec, vmem, smem, smem, any_spec, any_spec],
        out_specs=(vmem, vmem),
        scratch_shapes=scratch,
        compiler_params=pltpu.CompilerParams(
            collective_id=0, has_side_effects=True, vmem_limit_bytes=60 * 1024 * 1024
        ),
        name="cg_step",
    )(
        res, dirn, flat(jnp.transpose(legendre, (2, 0, 1))),
        jnp.transpose(beam_coef), prior_weight.reshape(ll // LANES, LANES), tile_ids, tile_ids,
        interp_weight[0], psi_angle[0], noise_coef, band_width, table, jnp.asarray(table_np.T) if two else table[:16],
    )
    outs = pl.pallas_call(
        update_kernel, out_shape=(flat_shape,) * 3, in_specs=[vmem] * 5, out_specs=(vmem,) * 3,
        name="cg_update",
    )(sol, res, dirn, image, sums)
    return tuple(unflat(o, 2, mo, ll) for o in outs)


def solution(mesh):
    nb, nd = mesh.shape["blk"], mesh.shape["det"]
    field = P(None, ("days", "blk"), "det")
    spans = ("days", "blk", "det")
    in_specs = (
        field, field, field, P("blk", "det", None), P("det", "beam"), P("det"), P(spans, None),
        P(spans, None, None, None), P(spans, None, None), P(spans, None, None), P(spans, None),
    )

    def run(*args):
        orders = args[2].shape[1] // (nb * mesh.shape["days"])
        table = padded_table(nb, orders)
        return jax.shard_map(
            functools.partial(body, nb, nd, table),
            mesh=mesh, in_specs=in_specs, out_specs=(field,) * 3, check_vma=False,
        )(*args)

    return run
```

```python
import functools
import math

import jax
import jax.numpy as jnp
import ml_dtypes
import numpy as np
from jax import lax
from jax.experimental import pallas as pl
from jax.experimental.pallas import tpu as pltpu
from jax.sharding import PartitionSpec as P

K = 16
P_SIZE = 2048
TPIX = 128
SPD = 1024
BW = 8
LANES = 128
HALF = 48
F32 = jnp.float32
BF16 = jnp.bfloat16
MESH = pl.DeviceIdType.MESH


def padded_table(blocks, orders):
    total = blocks * orders
    m = np.arange(total, dtype=np.int64)
    j = np.arange(P_SIZE, dtype=np.int64)
    phase = ((m[:, None] * j[None, :]) % P_SIZE).astype(np.float32) * np.float32(
        2.0 * math.pi / P_SIZE
    )
    scale = np.float32(1.0 / math.sqrt(2.0 * total))
    table = np.zeros((blocks, LANES, P_SIZE), np.float32)
    table[:, :orders] = (np.cos(phase) * scale).reshape(blocks, orders, P_SIZE)
    table[:, HALF : HALF + orders] = (-np.sin(phase) * scale).reshape(blocks, orders, P_SIZE)
    return table.reshape(blocks * LANES, P_SIZE).astype(ml_dtypes.bfloat16)


def loop(count, step):
    if count <= 8:
        for i in range(count):
            step(i)
    else:
        lax.fori_loop(0, count, lambda i, c: (step(i), c)[1], 0)


def mult(x, m):
    return x if isinstance(x, int) else pl.multiple_of(x, m)


def dot_nt(a, b):
    return lax.dot_general(a, b, (((1,), (1,)), ((), ())), preferred_element_type=F32)


def dot_nn(a, b):
    return lax.dot_general(a, b, (((1,), (0,)), ((), ())), preferred_element_type=F32)


def dot_tn(a, b):
    return lax.dot_general(a, b, (((0,), (0,)), ((), ())), preferred_element_type=F32)


def split2(x):
    hi = x.astype(BF16)
    return hi, (x - hi.astype(F32)).astype(BF16)


def kernel(
    nb, nd, mo, rr, kl, two, res_h, dir_h, leg_h, beam_v, prior_v, ids_s, ids_v, w_h, psi_v,
    noise_s, band_s, table_h, back_h, img, sums_v,
    res_v, dir_v, leg_v, legf, w_v, table_v, back_s, yhi, ylo, part, asend, arecv, coef, brecv,
    tiles, basis, prod, sigs, filt, sadj, tt, adj, dsend, drecv, erecv, backf, gsend, grecv,
    in_sem, b_sem, a_ss, a_rs, c_sem, d_ss, d_rs, e_ss, e_rs, g_ss, g_rs,
):
    n = nb * nd
    back_v = back_s if two else None
    days, blk = lax.axis_index("days"), lax.axis_index("blk")
    det, beam = lax.axis_index("det"), lax.axis_index("beam")
    me = blk * nd + det
    kr = rr * kl
    lt_n = beam_v.shape[1] // LANES
    slots = w_v.shape[0]
    tile_n = P_SIZE // TPIX

    def peer(i):
        if isinstance(i, int) and n & (n - 1) == 0:
            t = me
            for bit in [1 << q for q in range(n.bit_length() - 1) if (n - i) >> q & 1]:
                t = t + bit * (1 - 2 * lax.rem(lax.div(me, bit), 2))
        else:
            t = lax.rem(me + i, n)
        return t, lax.div(t, nd), lax.rem(t, nd)

    loads = [
        pltpu.make_async_copy(src, dst, in_sem.at[i])
        for i, (src, dst) in enumerate(
            [(dir_h, dir_v), (leg_h, leg_v), (table_h, table_v), (w_h, w_v), (res_h, res_v)]
        )
    ]
    if two:
        loads.append(pltpu.make_async_copy(back_h, back_s, in_sem.at[5]))
    for copy in loads:
        copy.start()

    barrier = pltpu.get_barrier_semaphore()

    def greet(i):
        _, b, d = peer(i + 1)
        pl.semaphore_signal(barrier, inc=1, device_id=(days, b, d, beam), device_id_type=MESH)

    loop(n - 1, greet)
    pl.semaphore_signal(barrier, inc=1, device_id=(days, blk, det, 1 - beam), device_id_type=MESH)

    def rows(start, stride):
        return pl.ds(start, mo, stride=stride)

    loads[0].wait()
    loads[1].wait()
    legf[...] = leg_v[...].astype(F32)
    brecv[beam] = beam_v[...]
    bh = beam_v[...].astype(BF16).astype(F32)
    lhs = jnp.concatenate([bh, beam_v[...] - bh], axis=0).astype(BF16)
    lane = lax.broadcasted_iota(jnp.int32, (kl, LANES), 1)
    keep = (lax.rem(lane, HALF) < mo) & (lane < 2 * HALF)

    def forward(pair):
        for h in range(2):
            r = pair * 2 + h
            for lt in range(lt_n):
                lg = legf[rows(lt * rr + r, lt_n * rr), :]
                for c in range(2):
                    y = dir_v[rows(lt * 2 + c, lt_n * 2), :] * lg
                    yh, yl = split2(y)
                    at = mult(r * LANES + c * HALF, 16)
                    yhi[pl.ds(at, mo), lt * LANES : (lt + 1) * LANES] = yh
                    ylo[pl.ds(at, mo), lt * LANES : (lt + 1) * LANES] = yl
        span = pl.ds(mult(pair * 2 * LANES, 2 * LANES), 2 * LANES)
        oh = dot_nt(yhi[span, :], lhs).T
        ol = dot_nt(ylo[span, :], lhs).T
        total = oh[:kl] + (oh[kl:] + ol[:kl])
        for h in range(2):
            at = mult((pair * 2 + h) * kl, kl)
            part[pl.ds(at, kl), :] = jnp.where(keep, total[:, h * LANES : (h + 1) * LANES], 0.0)

    loop(rr // 2, forward)
    asend[...] = part[...].astype(BF16)
    arecv[me] = asend[...]

    pl.semaphore_wait(barrier, n)

    def a_send(i):
        _, b, d = peer(i + 1)
        pltpu.make_async_remote_copy(
            asend, arecv.at[me], a_ss, a_rs, device_id=(days, b, d, beam), device_id_type=MESH
        ).start()

    loop(n - 1, a_send)
    sister = (days, blk, det, 1 - beam)
    b_copy = pltpu.make_async_remote_copy(
        beam_v, brecv.at[beam], b_sem.at[0], b_sem.at[1], device_id=sister, device_id_type=MESH
    )
    b_copy.start()

    sent = []

    def wait_all(buffer, send_sem, recv_sem):
        some = buffer.at[pl.ds(0, n - 1)]
        pltpu.make_async_copy(some, some, recv_sem).wait()
        sent.append((some, send_sem))

    psi = psi_v[...]
    c1, s1 = jnp.cos(psi), jnp.sin(psi)
    ck, sk = jnp.ones_like(psi), jnp.zeros_like(psi)
    first = beam == 0
    for k in range(kl):
        cn, sn = ck * c1 - sk * s1, sk * c1 + ck * s1
        basis[pl.ds(k, slots, stride=kl), :] = jnp.where(first, ck, sn)
        ck, sk = cn, sn

    wait_all(arecv, a_ss, a_rs)

    def add_det(b):
        total = arecv[b * nd].astype(F32)
        for d in range(1, nd):
            total = total + arecv[b * nd + d].astype(F32)
        coef[:, pl.ds(mult(b * LANES, LANES), LANES)] = total.astype(BF16)

    loop(nb, add_det)

    loads[2].wait()
    width = 512
    lhs_c = coef[...]

    def to_pixels(jc):
        out = dot_nn(lhs_c, table_v[:, pl.ds(mult(jc * width, width), width)])
        out = out.astype(BF16).astype(F32)
        for r in range(rr):
            for q in range(width // TPIX):
                tiles[r * tile_n + jc * (width // TPIX) + q] = out[
                    r * kl : (r + 1) * kl, q * TPIX : (q + 1) * TPIX
                ]

    loop(P_SIZE // width, to_pixels)
    loads[3].wait()
    for s in range(slots):
        tile = tiles[ids_s[0, s]].astype(BF16)
        at = slice(s * kl, (s + 1) * kl)
        prod[at, :] = basis[at, :] * dot_nt(tile, w_v[s])
    sig = prod[pl.ds(0, slots, stride=kl), :]
    for k in range(1, kl):
        sig = sig + prod[pl.ds(k, slots, stride=kl), :]
    sigs[beam] = sig
    c_copy = pltpu.make_async_remote_copy(
        sigs.at[beam], sigs.at[beam], c_sem.at[0], c_sem.at[1], device_id=sister, device_id_type=MESH
    )
    c_copy.start()
    c_copy.wait()

    srow = SPD // LANES
    row8 = lax.broadcasted_iota(jnp.int32, (srow, LANES), 0)
    lane8 = lax.broadcasted_iota(jnp.int32, (srow, LANES), 1)
    for d in range(slots // srow):
        at = slice(d * srow, (d + 1) * srow)
        x = sigs[0, at, :] + sigs[1, at, :]
        prev = jnp.where(row8 == 0, 0.0, pltpu.roll(x, 1, 0))
        nxt = jnp.where(row8 == srow - 1, 0.0, pltpu.roll(x, srow - 1, 0))
        center = jnp.float32(0.0)
        total = jnp.zeros_like(x)
        for i in range(1, BW + 1):
            tap = jnp.where(i <= band_s[0, d], noise_s[0, d, i - 1], 0.0)
            center = center + jnp.abs(tap)
            before = jnp.where(lane8 < i, pltpu.roll(prev, i, 1), pltpu.roll(x, i, 1))
            after = jnp.where(
                lane8 >= LANES - i, pltpu.roll(nxt, LANES - i, 1), pltpu.roll(x, LANES - i, 1)
            )
            total = total + tap * (before + after)
        filt[at, :] = (1.0 + 2.0 * center) * x + total

    for s in range(slots):
        at = slice(s * kl, (s + 1) * kl)
        wt = (basis[at, :] * filt[s : s + 1, :]).astype(BF16)
        sadj[at, :] = dot_nn(wt, w_v[s])
    tiles_all = rr * tile_n
    hot = (
        lax.broadcasted_iota(jnp.int32, (tiles_all, slots), 0) == ids_v[...]
    ).astype(F32).astype(BF16)
    xs = jnp.concatenate([sadj[pl.ds(k, slots, stride=kl), :] for k in range(kl)], axis=1)
    xh, xl = split2(xs)
    ts = dot_nn(hot, xh) + dot_nn(hot, xl)
    for k in range(kl):
        tt[pl.ds(k, tiles_all, stride=kl), :] = ts[:, k * TPIX : (k + 1) * TPIX]
    for r in range(rr):
        for q in range(tile_n):
            g = r * tile_n + q
            adj[r * kl : (r + 1) * kl, q * TPIX : (q + 1) * TPIX] = tt[g * kl : (g + 1) * kl, :]
    if two:
        loads[5].wait()
    ah, al = split2(adj[...])
    lhs_a = jnp.concatenate([ah, al], axis=0)

    def to_orders(pair):
        span = pl.ds(mult(pair * 2 * LANES, 2 * LANES), 2 * LANES)
        if back_v is None:
            out = dot_nt(lhs_a, table_v[span, :])
        else:
            out = dot_nn(lhs_a, back_v[:, span])
        out = out[:kr] + out[kr:]
        for h in range(2):
            dsend[pair * 2 + h] = out[:, h * LANES : (h + 1) * LANES].astype(BF16)

    loop(nb // 2, to_orders)

    def d_send(i):
        _, b, d = peer(i + 1)
        pltpu.make_async_remote_copy(
            dsend.at[b], drecv.at[me], d_ss, d_rs,
            device_id=(days, b, d, beam), device_id_type=MESH,
        ).start()

    loop(n - 1, d_send)
    drecv[me] = dsend[blk]
    wait_all(drecv, d_ss, d_rs)
    back = drecv[0].astype(F32)
    for i in range(1, n):
        back = back + drecv[i].astype(F32)
    erecv[beam] = back.astype(BF16)
    e_copies = [
        pltpu.make_async_remote_copy(
            erecv.at[beam], erecv.at[beam], e_ss, e_rs, device_id=sister, device_id_type=MESH
        )
    ]
    for copy in e_copies:
        copy.start()
    loads[4].wait()
    b_copy.wait()
    bm_all = jnp.concatenate([brecv[0], brecv[1]], axis=0)
    gh = bm_all.astype(BF16)
    rhs_b = jnp.concatenate([gh, (bm_all - gh.astype(F32)).astype(BF16)], axis=0)
    for copy in e_copies:
        copy.wait()
    for bm in range(2):
        backf[bm] = erecv[bm].astype(F32)

    def spread(r):
        at = pl.ds(mult(r * kl, kl), kl)
        b0, b1 = backf[0, at, :], backf[1, at, :]
        lb = jnp.concatenate([b0, b1, b0, b1], axis=0)[:, : 2 * HALF].astype(BF16)
        return dot_tn(lb, rhs_b)

    acc = None
    if rr <= 4:
        fields = [spread(r) for r in range(rr)]
    else:
        for q in range(lt_n * 2):
            at = rows(q, lt_n * 2)
            img[at, :] = jnp.zeros((mo, LANES), F32)

        def to_image(r):
            g = spread(r)
            for lt in range(lt_n):
                lg = legf[rows(lt * rr + r, lt_n * rr), :]
                for c in range(2):
                    to = rows(lt * 2 + c, lt_n * 2)
                    img[to, :] = img[to, :] + lg * g[
                        c * HALF : c * HALF + mo, lt * LANES : (lt + 1) * LANES
                    ]

        loop(rr, to_image)

    for lt in range(lt_n):
        if rr <= 4:
            lgs = [legf[rows(lt * rr + r, lt_n * rr), :] for r in range(rr)]
        for c in range(2):
            at = rows(lt * 2 + c, lt_n * 2)
            dv, rv = dir_v[at, :], res_v[at, :]
            iv = prior_v[lt : lt + 1, :] * dv
            if rr <= 4:
                for lg, g in zip(lgs, fields):
                    iv = iv + lg * g[c * HALF : c * HALF + mo, lt * LANES : (lt + 1) * LANES]
            else:
                iv = iv + img[at, :]
            img[at, :] = iv
            terms = [rv * rv, dv * iv, rv * iv, iv * iv]
            acc = terms if acc is None else [a + t for a, t in zip(acc, terms)]
    gsend[...] = jnp.zeros_like(gsend)
    for i, a in enumerate(acc):
        gsend[i : i + 1, :] = jnp.sum(a, axis=0, keepdims=True)

    def g_send(i):
        _, b, d = peer(i + 1)
        pltpu.make_async_remote_copy(
            gsend, grecv.at[me], g_ss, g_rs, device_id=(days, b, d, beam), device_id_type=MESH
        ).start()

    loop(n - 1, g_send)
    grecv[me] = gsend[...]
    wait_all(grecv, g_ss, g_rs)
    tot = grecv[0]
    for i in range(1, n):
        tot = tot + grecv[i]
    sums_v[...] = tot
    for some, sem in sent:
        pltpu.make_async_copy(some, some, sem).wait()


def update_kernel(sol_v, res_v, dir_v, img_v, sums_v, osol_v, ores_v, odir_v):
    sums = jnp.sum(sums_v[...], axis=1, keepdims=True)
    rr_sum, di_sum, ri_sum, ii_sum = (sums[i : i + 1, :] for i in range(4))
    alpha = rr_sum / di_sum
    new_norm = rr_sum - 2.0 * alpha * ri_sum + alpha * alpha * ii_sum
    beta = new_norm / rr_sum
    dv = dir_v[...]
    nr = res_v[...] - alpha * img_v[...]
    ores_v[...] = nr
    osol_v[...] = sol_v[...] + alpha * dv
    odir_v[...] = nr + beta * dv


def flat(x):
    a, m, l = x.shape
    y = jnp.transpose(x, (1, 0, 2)).reshape(m, a, l // LANES, LANES)
    return jnp.transpose(y, (0, 2, 1, 3)).reshape(m * l // LANES * a, LANES)


def unflat(y, a, m, l):
    x = jnp.transpose(y.reshape(m, l // LANES, a, LANES), (0, 2, 1, 3)).reshape(m, a, l)
    return jnp.transpose(x, (1, 0, 2))


def body(
    nb, nd, table_np, solution, residual, direction, legendre, beam_coef, prior_weight, tile_ids,
    interp_weight, psi_angle, noise_coef, band_width,
):
    _, mo, ll = direction.shape
    table = jnp.asarray(table_np)
    two = nb <= 8
    rr = legendre.shape[2]
    kl = beam_coef.shape[1]
    slots = tile_ids.shape[1]
    n = nb * nd
    kr = rr * kl
    frows = 2 * mo * ll // LANES
    lrows = rr * mo * ll // LANES
    tiles_all = rr * (P_SIZE // TPIX)
    any_spec = pl.BlockSpec(memory_space=pl.ANY)
    vmem = pl.BlockSpec(memory_space=pltpu.VMEM)
    smem = pl.BlockSpec(memory_space=pltpu.SMEM)
    V = pltpu.VMEM
    dma = pltpu.SemaphoreType.DMA
    flat_shape = jax.ShapeDtypeStruct((frows, LANES), F32)
    sol, res, dirn = flat(solution), flat(residual), flat(direction)
    scratch = [
        V((frows, LANES), F32), V((frows, LANES), F32),
        V((lrows, LANES), BF16), V((lrows, LANES), F32),
        V((slots, LANES, TPIX), BF16), V((nb * LANES, P_SIZE), BF16),
        V((P_SIZE, nb * LANES) if two else (16, LANES), BF16),
        V((rr * LANES, ll), BF16), V((rr * LANES, ll), BF16),
        V((kr, LANES), F32), V((kr, LANES), BF16), V((n, kr, LANES), BF16),
        V((kr, nb * LANES), BF16), V((2, kl, ll), F32),
        V((tiles_all, kl, TPIX), F32), V((slots * kl, LANES), F32), V((slots * kl, LANES), F32),
        V((2, slots, LANES), F32), V((slots, LANES), F32), V((slots * kl, TPIX), F32),
        V((tiles_all * kl, TPIX), F32), V((kr, P_SIZE), F32),
        V((nb, kr, LANES), BF16), V((n, kr, LANES), BF16),
        V((2, kr, LANES), BF16), V((2, kr, LANES), F32),
        V((8, LANES), F32), V((n, 8, LANES), F32),
        dma((6,)), dma((2,)), dma, dma, dma((2,)), dma, dma,
        dma, dma, dma, dma,
    ]
    held = sum(
        math.prod(v.shape) * v.dtype.itemsize for v in scratch if hasattr(v, 'dtype') and getattr(v, 'memory_space', None) == V)
    grant = held + held // 8 + 6 * 1024 * 1024
    image, sums = pl.pallas_call(
        functools.partial(kernel, nb, nd, mo, rr, kl, two),
        out_shape=(flat_shape, jax.ShapeDtypeStruct((8, LANES), F32)),
        in_specs=[any_spec] * 3 + [vmem, vmem, smem, vmem, any_spec, vmem, smem, smem, any_spec, any_spec],
        out_specs=(vmem, vmem),
        scratch_shapes=scratch,
        compiler_params=pltpu.CompilerParams(
            collective_id=0, has_side_effects=True, vmem_limit_bytes=60 * 1024 * 1024
        ),
        name="cg_step",
    )(
        res, dirn, flat(jnp.transpose(legendre, (2, 0, 1))),
        jnp.transpose(beam_coef), prior_weight.reshape(ll // LANES, LANES), tile_ids, tile_ids,
        interp_weight[0], psi_angle[0], noise_coef, band_width, table, jnp.asarray(table_np.T) if two else table[:16],
    )
    outs = pl.pallas_call(
        update_kernel, out_shape=(flat_shape,) * 3, in_specs=[vmem] * 5, out_specs=(vmem,) * 3,
        name="cg_update",
    )(sol, res, dirn, image, sums)
    return tuple(unflat(o, 2, mo, ll) for o in outs)


def solution(mesh):
    nb, nd = mesh.shape["blk"], mesh.shape["det"]
    field = P(None, ("days", "blk"), "det")
    spans = ("days", "blk", "det")
    in_specs = (
        field, field, field, P("blk", "det", None), P("det", "beam"), P("det"), P(spans, None),
        P(spans, None, None, None), P(spans, None, None), P(spans, None, None), P(spans, None),
    )

    def run(*args):
        orders = args[2].shape[1] // (nb * mesh.shape["days"])
        table = padded_table(nb, orders)
        return jax.shard_map(
            functools.partial(body, nb, nd, table),
            mesh=mesh, in_specs=in_specs, out_specs=(field,) * 3, check_vma=False,
        )(*args)

    return run
```

```python
import functools
import math

import jax
import jax.numpy as jnp
import ml_dtypes
import numpy as np
from jax import lax
from jax.experimental import pallas as pl
from jax.experimental.pallas import tpu as pltpu
from jax.sharding import PartitionSpec as P

K = 16
P_SIZE = 2048
TPIX = 128
SPD = 1024
BW = 8
LANES = 128
HALF = 48
F32 = jnp.float32
BF16 = jnp.bfloat16
MESH = pl.DeviceIdType.MESH


def padded_table(blocks, orders):
    total = blocks * orders
    m = np.arange(total, dtype=np.int64)
    j = np.arange(P_SIZE, dtype=np.int64)
    phase = ((m[:, None] * j[None, :]) % P_SIZE).astype(np.float32) * np.float32(
        2.0 * math.pi / P_SIZE
    )
    scale = np.float32(1.0 / math.sqrt(2.0 * total))
    table = np.zeros((blocks, LANES, P_SIZE), np.float32)
    table[:, :orders] = (np.cos(phase) * scale).reshape(blocks, orders, P_SIZE)
    table[:, HALF : HALF + orders] = (-np.sin(phase) * scale).reshape(blocks, orders, P_SIZE)
    return table.reshape(blocks * LANES, P_SIZE).astype(ml_dtypes.bfloat16)


def loop(count, step):
    if count <= 8:
        for i in range(count):
            step(i)
    else:
        lax.fori_loop(0, count, lambda i, c: (step(i), c)[1], 0)


def mult(x, m):
    return x if isinstance(x, int) else pl.multiple_of(x, m)


def dot_nt(a, b):
    return lax.dot_general(a, b, (((1,), (1,)), ((), ())), preferred_element_type=F32)


def dot_nn(a, b):
    return lax.dot_general(a, b, (((1,), (0,)), ((), ())), preferred_element_type=F32)


def dot_tn(a, b):
    return lax.dot_general(a, b, (((0,), (0,)), ((), ())), preferred_element_type=F32)


def split2(x):
    hi = x.astype(BF16)
    return hi, (x - hi.astype(F32)).astype(BF16)


def kernel(
    nb, nd, mo, rr, kl, two, res_h, dir_h, leg_h, beam_v, prior_v, ids_s, ids_v, w_h, psi_v,
    noise_s, band_s, table_h, back_h, img_h, sums_v,
    res_v, dir_v, leg_v, legf, w_v, table_v, back_s, yhi, ylo, part, asend, arecv, coef, brecv,
    tiles, basis, prod, sigs, filt, sadj, tt, adj, dsend, drecv, erecv, backf, img, gsend, grecv,
    in_sem, b_sem, a_ss, a_rs, c_sem, d_ss, d_rs, e_ss, e_rs, g_ss, g_rs, i_sem,
):
    n = nb * nd
    back_v = back_s if two else None
    days, blk = lax.axis_index("days"), lax.axis_index("blk")
    det, beam = lax.axis_index("det"), lax.axis_index("beam")
    me = blk * nd + det
    kr = rr * kl
    lt_n = beam_v.shape[1] // LANES
    slots = w_v.shape[0]
    tile_n = P_SIZE // TPIX

    def peer(i):
        if isinstance(i, int) and n & (n - 1) == 0:
            t = me
            for bit in [1 << q for q in range(n.bit_length() - 1) if (n - i) >> q & 1]:
                t = t + bit * (1 - 2 * lax.rem(lax.div(me, bit), 2))
        else:
            t = lax.rem(me + i, n)
        return t, lax.div(t, nd), lax.rem(t, nd)

    loads = [
        pltpu.make_async_copy(src, dst, in_sem.at[i])
        for i, (src, dst) in enumerate(
            [(dir_h, dir_v), (leg_h, leg_v), (table_h, table_v), (w_h, w_v), (res_h, res_v)]
        )
    ]
    if two:
        loads.append(pltpu.make_async_copy(back_h, back_s, in_sem.at[5]))
    for copy in loads:
        copy.start()

    barrier = pltpu.get_barrier_semaphore()

    def greet(i):
        _, b, d = peer(i + 1)
        pl.semaphore_signal(barrier, inc=1, device_id=(days, b, d, beam), device_id_type=MESH)

    loop(n - 1, greet)
    pl.semaphore_signal(barrier, inc=1, device_id=(days, blk, det, 1 - beam), device_id_type=MESH)

    def rows(start, stride):
        return pl.ds(start, mo, stride=stride)

    loads[0].wait()
    loads[1].wait()
    legf[...] = leg_v[...].astype(F32)
    brecv[beam] = beam_v[...]
    bh = beam_v[...].astype(BF16).astype(F32)
    lhs = jnp.concatenate([bh, beam_v[...] - bh], axis=0).astype(BF16)
    lane = lax.broadcasted_iota(jnp.int32, (kl, LANES), 1)
    keep = (lax.rem(lane, HALF) < mo) & (lane < 2 * HALF)

    def forward(pair):
        for h in range(2):
            r = pair * 2 + h
            for lt in range(lt_n):
                lg = legf[rows(lt * rr + r, lt_n * rr), :]
                for c in range(2):
                    y = dir_v[rows(lt * 2 + c, lt_n * 2), :] * lg
                    yh, yl = split2(y)
                    at = mult(r * LANES + c * HALF, 16)
                    yhi[pl.ds(at, mo), lt * LANES : (lt + 1) * LANES] = yh
                    ylo[pl.ds(at, mo), lt * LANES : (lt + 1) * LANES] = yl
        span = pl.ds(mult(pair * 2 * LANES, 2 * LANES), 2 * LANES)
        oh = dot_nt(yhi[span, :], lhs).T
        ol = dot_nt(ylo[span, :], lhs).T
        total = oh[:kl] + (oh[kl:] + ol[:kl])
        for h in range(2):
            at = mult((pair * 2 + h) * kl, kl)
            part[pl.ds(at, kl), :] = jnp.where(keep, total[:, h * LANES : (h + 1) * LANES], 0.0)

    loop(rr // 2, forward)
    asend[...] = part[...].astype(BF16)
    arecv[me] = asend[...]

    pl.semaphore_wait(barrier, n)

    def a_send(i):
        _, b, d = peer(i + 1)
        pltpu.make_async_remote_copy(
            asend, arecv.at[me], a_ss, a_rs, device_id=(days, b, d, beam), device_id_type=MESH
        ).start()

    loop(n - 1, a_send)
    sister = (days, blk, det, 1 - beam)
    b_copy = pltpu.make_async_remote_copy(
        beam_v, brecv.at[beam], b_sem.at[0], b_sem.at[1], device_id=sister, device_id_type=MESH
    )
    b_copy.start()

    sent = []

    def wait_all(buffer, send_sem, recv_sem):
        some = buffer.at[pl.ds(0, n - 1)]
        pltpu.make_async_copy(some, some, recv_sem).wait()
        sent.append((some, send_sem))

    psi = psi_v[...]
    c1, s1 = jnp.cos(psi), jnp.sin(psi)
    ck, sk = jnp.ones_like(psi), jnp.zeros_like(psi)
    first = beam == 0
    for k in range(kl):
        cn, sn = ck * c1 - sk * s1, sk * c1 + ck * s1
        basis[pl.ds(k, slots, stride=kl), :] = jnp.where(first, ck, sn)
        ck, sk = cn, sn

    wait_all(arecv, a_ss, a_rs)

    def add_det(b):
        total = arecv[b * nd].astype(F32)
        for d in range(1, nd):
            total = total + arecv[b * nd + d].astype(F32)
        coef[:, pl.ds(mult(b * LANES, LANES), LANES)] = total.astype(BF16)

    loop(nb, add_det)

    loads[2].wait()
    width = 512
    lhs_c = coef[...]

    def to_pixels(jc):
        out = dot_nn(lhs_c, table_v[:, pl.ds(mult(jc * width, width), width)])
        out = out.astype(BF16).astype(F32)
        for r in range(rr):
            for q in range(width // TPIX):
                tiles[r * tile_n + jc * (width // TPIX) + q] = out[
                    r * kl : (r + 1) * kl, q * TPIX : (q + 1) * TPIX
                ]

    loop(P_SIZE // width, to_pixels)
    loads[3].wait()
    for s in range(slots):
        tile = tiles[ids_s[0, s]].astype(BF16)
        at = slice(s * kl, (s + 1) * kl)
        prod[at, :] = basis[at, :] * dot_nt(tile, w_v[s])
    sig = prod[pl.ds(0, slots, stride=kl), :]
    for k in range(1, kl):
        sig = sig + prod[pl.ds(k, slots, stride=kl), :]
    sigs[beam] = sig
    c_copy = pltpu.make_async_remote_copy(
        sigs.at[beam], sigs.at[beam], c_sem.at[0], c_sem.at[1], device_id=sister, device_id_type=MESH
    )
    c_copy.start()
    c_copy.wait()

    srow = SPD // LANES
    row8 = lax.broadcasted_iota(jnp.int32, (srow, LANES), 0)
    lane8 = lax.broadcasted_iota(jnp.int32, (srow, LANES), 1)
    for d in range(slots // srow):
        at = slice(d * srow, (d + 1) * srow)
        x = sigs[0, at, :] + sigs[1, at, :]
        prev = jnp.where(row8 == 0, 0.0, pltpu.roll(x, 1, 0))
        nxt = jnp.where(row8 == srow - 1, 0.0, pltpu.roll(x, srow - 1, 0))
        center = jnp.float32(0.0)
        total = jnp.zeros_like(x)
        for i in range(1, BW + 1):
            tap = jnp.where(i <= band_s[0, d], noise_s[0, d, i - 1], 0.0)
            center = center + jnp.abs(tap)
            before = jnp.where(lane8 < i, pltpu.roll(prev, i, 1), pltpu.roll(x, i, 1))
            after = jnp.where(
                lane8 >= LANES - i, pltpu.roll(nxt, LANES - i, 1), pltpu.roll(x, LANES - i, 1)
            )
            total = total + tap * (before + after)
        filt[at, :] = (1.0 + 2.0 * center) * x + total

    for s in range(slots):
        at = slice(s * kl, (s + 1) * kl)
        wt = (basis[at, :] * filt[s : s + 1, :]).astype(BF16)
        sadj[at, :] = dot_nn(wt, w_v[s])
    tiles_all = rr * tile_n
    hot = (
        lax.broadcasted_iota(jnp.int32, (tiles_all, slots), 0) == ids_v[...]
    ).astype(F32).astype(BF16)
    xs = jnp.concatenate([sadj[pl.ds(k, slots, stride=kl), :] for k in range(kl)], axis=1)
    xh, xl = split2(xs)
    ts = dot_nn(hot, xh) + dot_nn(hot, xl)
    for k in range(kl):
        tt[pl.ds(k, tiles_all, stride=kl), :] = ts[:, k * TPIX : (k + 1) * TPIX]
    for r in range(rr):
        for q in range(tile_n):
            g = r * tile_n + q
            adj[r * kl : (r + 1) * kl, q * TPIX : (q + 1) * TPIX] = tt[g * kl : (g + 1) * kl, :]
    if two:
        loads[5].wait()
    ah, al = split2(adj[...])
    lhs_a = jnp.concatenate([ah, al], axis=0)

    def to_orders(pair):
        span = pl.ds(mult(pair * 2 * LANES, 2 * LANES), 2 * LANES)
        if back_v is None:
            out = dot_nt(lhs_a, table_v[span, :])
        else:
            out = dot_nn(lhs_a, back_v[:, span])
        out = out[:kr] + out[kr:]
        for h in range(2):
            dsend[pair * 2 + h] = out[:, h * LANES : (h + 1) * LANES].astype(BF16)

    loop(nb // 2, to_orders)

    def d_send(i):
        _, b, d = peer(i + 1)
        pltpu.make_async_remote_copy(
            dsend.at[b], drecv.at[me], d_ss, d_rs,
            device_id=(days, b, d, beam), device_id_type=MESH,
        ).start()

    loop(n - 1, d_send)
    drecv[me] = dsend[blk]
    wait_all(drecv, d_ss, d_rs)
    back = drecv[0].astype(F32)
    for i in range(1, n):
        back = back + drecv[i].astype(F32)
    erecv[beam] = back.astype(BF16)
    e_copies = [
        pltpu.make_async_remote_copy(
            erecv.at[beam], erecv.at[beam], e_ss, e_rs, device_id=sister, device_id_type=MESH
        )
    ]
    for copy in e_copies:
        copy.start()
    loads[4].wait()
    b_copy.wait()
    bm_all = jnp.concatenate([brecv[0], brecv[1]], axis=0)
    gh = bm_all.astype(BF16)
    rhs_b = jnp.concatenate([gh, (bm_all - gh.astype(F32)).astype(BF16)], axis=0)
    for copy in e_copies:
        copy.wait()
    for bm in range(2):
        backf[bm] = erecv[bm].astype(F32)

    def spread(r):
        at = pl.ds(mult(r * kl, kl), kl)
        b0, b1 = backf[0, at, :], backf[1, at, :]
        lb = jnp.concatenate([b0, b1, b0, b1], axis=0)[:, : 2 * HALF].astype(BF16)
        return dot_tn(lb, rhs_b)

    acc = None
    if rr <= 4:
        fields = [spread(r) for r in range(rr)]
    else:
        for q in range(lt_n * 2):
            at = rows(q, lt_n * 2)
            img[at, :] = jnp.zeros((mo, LANES), F32)

        def to_image(r):
            g = spread(r)
            for lt in range(lt_n):
                lg = legf[rows(lt * rr + r, lt_n * rr), :]
                for c in range(2):
                    to = rows(lt * 2 + c, lt_n * 2)
                    img[to, :] = img[to, :] + lg * g[
                        c * HALF : c * HALF + mo, lt * LANES : (lt + 1) * LANES
                    ]

        loop(rr, to_image)

    for lt in range(lt_n):
        if rr <= 4:
            lgs = [legf[rows(lt * rr + r, lt_n * rr), :] for r in range(rr)]
        for c in range(2):
            at = rows(lt * 2 + c, lt_n * 2)
            dv, rv = dir_v[at, :], res_v[at, :]
            iv = prior_v[lt : lt + 1, :] * dv
            if rr <= 4:
                for lg, g in zip(lgs, fields):
                    iv = iv + lg * g[c * HALF : c * HALF + mo, lt * LANES : (lt + 1) * LANES]
            else:
                iv = iv + img[at, :]
            img[at, :] = iv
            terms = [rv * rv, dv * iv, rv * iv, iv * iv]
            acc = terms if acc is None else [a + t for a, t in zip(acc, terms)]
    gsend[...] = jnp.zeros_like(gsend)
    for i, a in enumerate(acc):
        gsend[i : i + 1, :] = jnp.sum(a, axis=0, keepdims=True)

    def g_send(i):
        _, b, d = peer(i + 1)
        pltpu.make_async_remote_copy(
            gsend, grecv.at[me], g_ss, g_rs, device_id=(days, b, d, beam), device_id_type=MESH
        ).start()

    loop(n - 1, g_send)
    i_copy = pltpu.make_async_copy(img, img_h, i_sem)
    i_copy.start()
    grecv[me] = gsend[...]
    wait_all(grecv, g_ss, g_rs)
    tot = grecv[0]
    for i in range(1, n):
        tot = tot + grecv[i]
    sums_v[...] = tot
    i_copy.wait()
    for some, sem in sent:
        pltpu.make_async_copy(some, some, sem).wait()


def update_kernel(sol_v, res_v, dir_v, img_v, sums_v, osol_v, ores_v, odir_v):
    sums = jnp.sum(sums_v[...], axis=1, keepdims=True)
    rr_sum, di_sum, ri_sum, ii_sum = (sums[i : i + 1, :] for i in range(4))
    alpha = rr_sum / di_sum
    new_norm = rr_sum - 2.0 * alpha * ri_sum + alpha * alpha * ii_sum
    beta = new_norm / rr_sum
    dv = dir_v[...]
    nr = res_v[...] - alpha * img_v[...]
    ores_v[...] = nr
    osol_v[...] = sol_v[...] + alpha * dv
    odir_v[...] = nr + beta * dv


def flat(x):
    a, m, l = x.shape
    y = jnp.transpose(x, (1, 0, 2)).reshape(m, a, l // LANES, LANES)
    return jnp.transpose(y, (0, 2, 1, 3)).reshape(m * l // LANES * a, LANES)


def unflat(y, a, m, l):
    x = jnp.transpose(y.reshape(m, l // LANES, a, LANES), (0, 2, 1, 3)).reshape(m, a, l)
    return jnp.transpose(x, (1, 0, 2))


def body(
    nb, nd, table_np, solution, residual, direction, legendre, beam_coef, prior_weight, tile_ids,
    interp_weight, psi_angle, noise_coef, band_width,
):
    _, mo, ll = direction.shape
    table = jnp.asarray(table_np)
    two = nb <= 8
    rr = legendre.shape[2]
    kl = beam_coef.shape[1]
    slots = tile_ids.shape[1]
    n = nb * nd
    kr = rr * kl
    frows = 2 * mo * ll // LANES
    lrows = rr * mo * ll // LANES
    tiles_all = rr * (P_SIZE // TPIX)
    any_spec = pl.BlockSpec(memory_space=pl.ANY)
    vmem = pl.BlockSpec(memory_space=pltpu.VMEM)
    smem = pl.BlockSpec(memory_space=pltpu.SMEM)
    V = pltpu.VMEM
    dma = pltpu.SemaphoreType.DMA
    flat_shape = jax.ShapeDtypeStruct((frows, LANES), F32)
    sol, res, dirn = flat(solution), flat(residual), flat(direction)
    scratch = [
        V((frows, LANES), F32), V((frows, LANES), F32),
        V((lrows, LANES), BF16), V((lrows, LANES), F32),
        V((slots, LANES, TPIX), BF16), V((nb * LANES, P_SIZE), BF16),
        V((P_SIZE, nb * LANES) if two else (16, LANES), BF16),
        V((rr * LANES, ll), BF16), V((rr * LANES, ll), BF16),
        V((kr, LANES), F32), V((kr, LANES), BF16), V((n, kr, LANES), BF16),
        V((kr, nb * LANES), BF16), V((2, kl, ll), F32),
        V((tiles_all, kl, TPIX), F32), V((slots * kl, LANES), F32), V((slots * kl, LANES), F32),
        V((2, slots, LANES), F32), V((slots, LANES), F32), V((slots * kl, TPIX), F32),
        V((tiles_all * kl, TPIX), F32), V((kr, P_SIZE), F32),
        V((nb, kr, LANES), BF16), V((n, kr, LANES), BF16),
        V((2, kr, LANES), BF16), V((2, kr, LANES), F32),
        V((frows, LANES), F32), V((8, LANES), F32), V((n, 8, LANES), F32),
        dma((6,)), dma((2,)), dma, dma, dma((2,)), dma, dma,
        dma, dma, dma, dma, dma,
    ]
    held = sum(
        math.prod(v.shape) * v.dtype.itemsize for v in scratch if hasattr(v, 'dtype') and getattr(v, 'memory_space', None) == V)
    grant = held + held // 8 + 6 * 1024 * 1024
    image, sums = pl.pallas_call(
        functools.partial(kernel, nb, nd, mo, rr, kl, two),
        out_shape=(flat_shape, jax.ShapeDtypeStruct((8, LANES), F32)),
        in_specs=[any_spec] * 3 + [vmem, vmem, smem, vmem, any_spec, vmem, smem, smem, any_spec, any_spec],
        out_specs=(any_spec, vmem),
        scratch_shapes=scratch,
        compiler_params=pltpu.CompilerParams(
            collective_id=0, has_side_effects=True, vmem_limit_bytes=60 * 1024 * 1024
        ),
        name="cg_step",
    )(
        res, dirn, flat(jnp.transpose(legendre, (2, 0, 1))),
        jnp.transpose(beam_coef), prior_weight.reshape(ll // LANES, LANES), tile_ids, tile_ids,
        interp_weight[0], psi_angle[0], noise_coef, band_width, table, jnp.asarray(table_np.T) if two else table[:16],
    )
    outs = pl.pallas_call(
        update_kernel, out_shape=(flat_shape,) * 3, in_specs=[vmem] * 5, out_specs=(vmem,) * 3,
        name="cg_update",
    )(sol, res, dirn, image, sums)
    return tuple(unflat(o, 2, mo, ll) for o in outs)


def solution(mesh):
    nb, nd = mesh.shape["blk"], mesh.shape["det"]
    field = P(None, ("days", "blk"), "det")
    spans = ("days", "blk", "det")
    in_specs = (
        field, field, field, P("blk", "det", None), P("det", "beam"), P("det"), P(spans, None),
        P(spans, None, None, None), P(spans, None, None), P(spans, None, None), P(spans, None),
    )

    def run(*args):
        orders = args[2].shape[1] // (nb * mesh.shape["days"])
        table = padded_table(nb, orders)
        return jax.shard_map(
            functools.partial(body, nb, nd, table),
            mesh=mesh, in_specs=in_specs, out_specs=(field,) * 3, check_vma=False,
        )(*args)

    return run
```
